128 devices in a mesh: dp: 4 (over x), section: 2 (over core), ts: 16 (over z, y).
Axes of the slice: x: 4, y: 4, z: 4, core: 2. Of those that a mesh axis runs over, the one named last changes fastest.
Arguments:
- inputs: bfloat16 [2, 512, 4096], P(None, ('dp', 'ts')), may hold values from -6 to 6
- cotangent: bfloat16 [2, 512, 4096], P(None, ('dp', 'ts')), may hold values from -4 to 4
- gains: float32 [2, 4096], P('section'), may hold values from 0.1 to 1.9
- weights: bfloat16 [2, 3, 112, 12, 128, 128], P('section', None, 'ts'), may hold values from -0.1875 to 0.1875
- block_rows: int32 [2, 3, 112, 12], P('section', None, 'ts'), may hold values from 0 to 31, as said below
- block_count: int32 [2, 3, 112], P('section', None, 'ts'), may hold values from 4 to 12, as said below
Outputs:
- segment_outputs: bfloat16 [2, 2, 512, 4096], P('section', None, ('dp', 'ts'))
- input_grads: bfloat16 [2, 2, 512, 4096], P('section', None, ('dp', 'ts'))
- weight_grads: bfloat16 [2, 3, 112, 12, 128, 128], P('section', None, 'ts', None, 'dp')
The draws below stay inside these ranges and needn't reach their ends.
Inputs may be any that keep to these rules, and one draw needn't show every extreme that they name: `block_rows`: within the 12 slots of one hidden block of one matrix and segment the feature blocks are distinct. `block_count`: for every segment, matrix and index of ts some hidden block has all 12 slots live.
All inputs are finite; a program needn't handle non-finite values.
Results may differ from the reference program's by a relative error of at most 0.03.
Values may be sent and summed in bfloat16 or wider, within the bound.
A program may use at most 192 MiB of HBM per device.

```python
import jax
import jax.numpy as jnp
from jax import lax

D = 4096
BLOCK = 128
MICRO = 2
MB_TOK = 128
DBLOCKS = 32
HBLOCKS = 112
HB_DEV = 7
SLOTS = 12
TOKENS = 512
N_DP = 4
N_SECTION = 2
N_TS = 16


def draw_block_rows(key, part):
    key = jax.random.fold_in(key, 11)
    total_lists = N_SECTION * 3 * HBLOCKS
    keys = jax.random.split(key, total_lists)
    picks = jax.vmap(lambda single: jax.random.permutation(single, DBLOCKS)[:SLOTS])(keys)
    return picks.reshape(N_SECTION, 3, HBLOCKS, SLOTS).astype(jnp.int32)


def draw_block_count(key, part):
    key = jax.random.fold_in(key, 23)
    first_key, second_key = jax.random.split(key)
    lowest = DBLOCKS // 2 - SLOTS
    counts = jax.random.randint(first_key, (N_SECTION, 3, N_TS, HB_DEV), lowest, SLOTS + 1)
    full_at = jax.random.randint(second_key, (N_SECTION, 3, N_TS, 1), 0, HB_DEV)
    counts = jnp.where(jnp.arange(HB_DEV)[None, None, None, :] == full_at, SLOTS, counts)
    return counts.reshape(N_SECTION, 3, HBLOCKS).astype(jnp.int32)


def levels(stream_key, dims, shards, smallest, high):
    level, own = 1.0, jax.random.fold_in(stream_key, 6)
    for axis_at, shards_of in shards:
        draws = jnp.exp(jax.random.uniform(jax.random.fold_in(own, axis_at), (shards_of,), jnp.float32, smallest / len(shards), high / len(shards)))
        level = level * jnp.repeat(draws, dims[axis_at] // shards_of).reshape([-1 if axis == axis_at else 1 for axis in range(len(dims))])
    return level


def noise(rng, extent, deviation, limit, shards=(), kind=jnp.bfloat16):
    entries = jax.random.normal(rng, extent, jnp.float32) * deviation
    if len(shards) > 0:
        entries = levels(rng, extent, shards, -0.22, 0.18) * entries
    return jnp.clip(entries, min=-limit, max=limit).astype(kind)


def setup_inputs(seed: int = 0) -> dict:
    streams_of = jax.random.split(jax.random.key(seed), 7)
    return {
        "inputs": noise(streams_of[0], (MICRO, TOKENS, D), 1.0, 6.0, ((1, 64),)),
        "cotangent": noise(streams_of[1], (MICRO, TOKENS, D), 0.25, 4.0, ((1, 64),)),
        "gains": jnp.clip(1.0 + 0.18 * jax.random.normal(streams_of[2], (N_SECTION, D), jnp.float32), 0.1, 1.9),
        "weights": noise(streams_of[3], (N_SECTION, 3, HBLOCKS, SLOTS, BLOCK, BLOCK), (D // 4) ** -0.5, 0.1875, ((0, 2), (2, 16))),
        "block_rows": draw_block_rows(jax.random.fold_in(streams_of[6], 71), 0),
        "block_count": draw_block_count(jax.random.fold_in(streams_of[6], 71), 0),
    }


EPSILON = 1e-05

def normalize(values, gain):
    scale = lax.rsqrt(lax.optimization_barrier(jnp.mean(values * values, axis=-1, keepdims=True)) + EPSILON)
    return (scale, (values * scale * gain).astype(jnp.bfloat16))

def shard_parts(normed, blocks_w, lists, counts):
    rows_tok = normed.shape[0]
    live = (jnp.arange(SLOTS)[None, None, :] < counts[:, :, None]).astype(jnp.float32)
    masked = blocks_w.astype(jnp.float32) * live[..., None, None]
    onehot = (lists[..., None] == jnp.arange(DBLOCKS)[None, None, None, :]).astype(jnp.float32)
    feats = normed.astype(jnp.float32).reshape(rows_tok, DBLOCKS, BLOCK)
    x_gate = feats[:, lists[0]]
    x_up = feats[:, lists[1]]
    gate = jnp.einsum('rcjb,cjbn->rcn', x_gate, masked[0])
    upper = jnp.einsum('rcjb,cjbn->rcn', x_up, masked[1])
    hidden = (jax.nn.silu(gate) * upper).astype(jnp.bfloat16)
    return (live, masked, onehot, x_gate, x_up, gate, upper, hidden)

def shard_forward(normed, blocks_w, lists, counts):
    live, masked, onehot, x_gate, x_up, gate, upper, hidden = shard_parts(normed, blocks_w, lists, counts)
    product = jnp.einsum('rch,cjhd->rcjd', hidden.astype(jnp.float32), masked[2])
    branch = jnp.einsum('rcjd,cjk->rkd', product, onehot[2], precision=lax.Precision.HIGHEST)
    return branch.reshape(normed.shape[0], D).astype(jnp.bfloat16)

def shard_backward(normed, delta, blocks_w, lists, counts):
    live, masked, onehot, x_gate, x_up, gate, upper, hidden = shard_parts(normed, blocks_w, lists, counts)
    rows_tok = normed.shape[0]
    grad_blocks = delta.astype(jnp.float32).reshape(rows_tok, DBLOCKS, BLOCK)[:, lists[2]]
    d_hidden = jnp.einsum('rcjd,cjhd->rch', grad_blocks, masked[2])
    sig = jax.nn.sigmoid(gate)
    d_gate = (d_hidden * upper * sig * (1.0 + gate * (1.0 - sig))).astype(jnp.bfloat16)
    d_up = (d_hidden * gate * sig).astype(jnp.bfloat16)
    prod_gate = jnp.einsum('rcn,cjbn->rcjb', d_gate.astype(jnp.float32), masked[0])
    prod_up = jnp.einsum('rcn,cjbn->rcjb', d_up.astype(jnp.float32), masked[1])
    back = jnp.einsum('rcjb,cjk->rkb', prod_gate, onehot[0], precision=lax.Precision.HIGHEST)
    back = back + jnp.einsum('rcjb,cjk->rkb', prod_up, onehot[1], precision=lax.Precision.HIGHEST)
    grads = jnp.stack([jnp.einsum('rcjb,rcn->cjbn', x_gate, d_gate.astype(jnp.float32)), jnp.einsum('rcjb,rcn->cjbn', x_up, d_up.astype(jnp.float32)), jnp.einsum('rch,rcjd->cjhd', hidden.astype(jnp.float32), grad_blocks)]) * live[..., None, None]
    return (back.reshape(rows_tok, D).astype(jnp.bfloat16), grads)

def replica(tokens, delta_last, gains, weights, block_rows, block_count):
    shard_ids = jnp.arange(N_TS, dtype=jnp.int32)
    states = []
    normeds = []
    outputs = []
    act = tokens
    for layer in range(N_SECTION):
        values = act.astype(jnp.float32)
        scale, normed = normalize(values, gains[layer])

        def one_shard(shard, layer=layer, normed=normed):
            start = shard * HB_DEV
            return shard_forward(normed, lax.dynamic_slice_in_dim(weights[layer], start, HB_DEV, 1), lax.dynamic_slice_in_dim(block_rows[layer], start, HB_DEV, 1), lax.dynamic_slice_in_dim(block_count[layer], start, HB_DEV, 1))
        parts = lax.map(one_shard, shard_ids)
        act = (values + lax.optimization_barrier(jnp.sum(parts.astype(jnp.float32), axis=0))).astype(jnp.bfloat16)
        states.append(values)
        normeds.append(normed)
        outputs.append(act)
    delta = delta_last
    grads_list = [None] * N_SECTION
    input_list = [None] * N_SECTION
    for layer in reversed(range(N_SECTION)):

        def back_shard(shard, layer=layer, delta=delta):
            start = shard * HB_DEV
            return shard_backward(normeds[layer], delta, lax.dynamic_slice_in_dim(weights[layer], start, HB_DEV, 1), lax.dynamic_slice_in_dim(block_rows[layer], start, HB_DEV, 1), lax.dynamic_slice_in_dim(block_count[layer], start, HB_DEV, 1))
        backs, grads = lax.map(back_shard, shard_ids)
        d_norm = lax.optimization_barrier(jnp.sum(backs.astype(jnp.float32), axis=0))
        values = states[layer]
        scale, unused = normalize(values, gains[layer])
        cube = scale * scale * scale
        delta = (delta.astype(jnp.float32) + scale * gains[layer] * d_norm - values * cube * lax.optimization_barrier(jnp.mean(gains[layer] * d_norm * values, axis=-1, keepdims=True))).astype(jnp.bfloat16)
        input_list[layer] = delta
        grads_list[layer] = grads.transpose(1, 0, 2, 3, 4, 5).reshape(3, HBLOCKS, SLOTS, BLOCK, BLOCK)
    return (jnp.stack(outputs), jnp.stack(input_list), jnp.stack(grads_list))

def reference(inputs, cotangent, gains, weights, block_rows, block_count):
    per_rep = MICRO * MB_TOK
    tokens = inputs.reshape(MICRO, N_DP, MB_TOK, D).transpose(1, 0, 2, 3).reshape(N_DP, per_rep, D)
    deltas = cotangent.reshape(MICRO, N_DP, MB_TOK, D).transpose(1, 0, 2, 3).reshape(N_DP, per_rep, D)

    def step(total, pair):
        outs, ins, grads = replica(pair[0], pair[1], gains, weights, block_rows, block_count)
        return (total + grads.astype(jnp.bfloat16).astype(jnp.float32), (outs, ins))
    start = jnp.zeros((N_SECTION, 3, HBLOCKS, SLOTS, BLOCK, BLOCK), jnp.float32)
    total, (outs, ins) = lax.scan(step, start, (tokens, deltas))

    def arrange(values):
        values = values.reshape(N_DP, N_SECTION, MICRO, MB_TOK, D).transpose(1, 2, 0, 3, 4)
        return values.reshape(N_SECTION, MICRO, N_DP * MB_TOK, D)
    return (arrange(outs), arrange(ins), total.astype(jnp.bfloat16))
```

```python
import functools
import math

import jax
import jax.numpy as jnp
from jax import lax
from jax.experimental import pallas as pl
from jax.experimental.pallas import tpu as pltpu
from jax.sharding import PartitionSpec as P

EPSILON = 1e-05
MESH = pl.DeviceIdType.MESH
F32 = jnp.float32
BF16 = jnp.bfloat16
NT = (((1,), (1,)), ((), ()))


def kernel(
    side, n_dp,
    x_ref, cot_ref, gain_ref, w_hbm, inv_ref, rows_ref, live_ref,
    seg_ref, ing_ref, wg_ref,
    raw0, raw1, raw2, wgu, wd, g, part, rs1, rs2, mid, hop, gu, dhid, hid, hid_t, dgu, xt, db, ex1, ex2,
    w_sem, ag_send, ag_recv, rs_send, rs_recv, hop_send, hop_recv, ex_send, ex_recv,
):
    rows, width = x_ref.shape
    half = width // 2
    _, hb, slots, block, _ = w_hbm.shape
    kb = width // block
    tokens = side * side * rows
    quarter = block // n_dp
    sec = lax.axis_index("section")
    ts = lax.axis_index("ts")
    me = lax.axis_index("dp")
    z, y = ts // side, lax.rem(ts, side)
    right, left = lax.rem(me + 1, n_dp), lax.rem(me + n_dp - 1, n_dp)
    across = lax.rem(me + 2, n_dp)
    raw = (raw0, raw1, raw2)
    cols = (slice(0, half), slice(half, width))
    peers = [
        (lax.rem(z + d, side), lax.rem(y + d, side)) for d in range(1, side)
    ]

    w_copies = [
        pltpu.make_async_copy(w_hbm.at[m], raw[m].at[:, pl.ds(0, slots)], w_sem.at[m])
        for m in range(3)
    ]
    for copy in w_copies:
        copy.start()

    barrier = pltpu.get_barrier_semaphore()
    for pz, py in peers:
        pl.semaphore_signal(barrier, inc=1, device_id={"ts": pz * side + y}, device_id_type=MESH)
        pl.semaphore_signal(barrier, inc=1, device_id={"ts": z * side + py}, device_id_type=MESH)
    pl.semaphore_signal(barrier, inc=1, device_id={"dp": right}, device_id_type=MESH)
    pl.semaphore_signal(barrier, inc=1, device_id={"dp": left}, device_id_type=MESH)
    pl.semaphore_signal(barrier, inc=1, device_id={"section": 1 - sec}, device_id_type=MESH)
    pl.semaphore_wait(barrier, 2 * (side - 1) + 3)

    def remote(src, dst, send, recv, where):
        return pltpu.make_async_remote_copy(
            src_ref=src, dst_ref=dst, send_sem=send, recv_sem=recv,
            device_id=where, device_id_type=MESH,
        )

    def gather_copies(i, phase, part_of):
        copies = []
        for d, (pz, py) in enumerate(peers):
            if phase == 0:
                ref = g.at[i, z, y, :, cols[part_of]]
            elif part_of == 0:
                ref = g.at[i, z, :, :, cols[0]]
            else:
                ref = g.at[i, :, y, :, cols[1]]
            along_y = phase == part_of
            where = {"ts": z * side + py} if along_y else {"ts": pz * side + y}
            at = phase * 2 + part_of
            copies.append(remote(ref, ref, ag_send.at[i, at, d], ag_recv.at[i, at, d], where))
        return copies

    def gather_first(i):
        for part_of in (0, 1):
            for copy in gather_copies(i, 0, part_of):
                copy.start()

    def gather_second(i):
        for part_of in (0, 1):
            for copy in gather_copies(i, 0, part_of):
                copy.wait_recv()
            for copy in gather_copies(i, 1, part_of):
                copy.start()

    def gather_end(i):
        for part_of in (0, 1):
            for copy in gather_copies(i, 1, part_of):
                copy.wait_recv()
        for phase in (0, 1):
            for part_of in (0, 1):
                for copy in gather_copies(i, phase, part_of):
                    copy.wait_send()

    def scatter_copies(use, phase, part_of):
        copies = []
        for d, (pz, py) in enumerate(peers):
            if phase == 0 and part_of == 0:
                src, where = part.at[pz, :, :, cols[0]], {"ts": pz * side + y}
            elif phase == 0:
                src, where = part.at[:, py, :, cols[1]], {"ts": z * side + py}
            elif part_of == 0:
                src, where = mid.at[0, py], {"ts": z * side + py}
            else:
                src, where = mid.at[1, pz], {"ts": pz * side + y}
            dst = (rs1 if phase == 0 else rs2).at[use, part_of, d]
            at = phase * 2 + part_of
            copies.append(remote(src, dst, rs_send.at[use, at, d], rs_recv.at[use, at, d], where))
        return copies

    def scatter_start(use, part_of):
        for copy in scatter_copies(use, 0, part_of):
            copy.start()

    def scatter_middle(use):
        for part_of in (0, 1):
            for copy in scatter_copies(use, 0, part_of):
                copy.wait_recv()
            for i in range(side):
                own = part[z, i, :, cols[0]] if part_of == 0 else part[i, y, :, cols[1]]
                total = own.astype(F32)
                for d in range(side - 1):
                    total = total + rs1[use, part_of, d, i].astype(F32)
                mid[part_of, i] = total.astype(BF16)
            for copy in scatter_copies(use, 1, part_of):
                copy.start()

    def scatter_end(use):
        totals = []
        for part_of in (0, 1):
            for copy in scatter_copies(use, 1, part_of):
                copy.wait_recv()
            total = mid[part_of, y if part_of == 0 else z].astype(F32)
            for d in range(side - 1):
                total = total + rs2[use, part_of, d].astype(F32)
            totals.append(total)
        for phase in (0, 1):
            for part_of in (0, 1):
                for copy in scatter_copies(use, phase, part_of):
                    copy.wait_send()
        return jnp.concatenate(totals, axis=1)

    def scale_of(values):
        return lax.rsqrt(jnp.mean(values * values, axis=-1, keepdims=True) + EPSILON)

    def normed_of(values):
        return (values * scale_of(values) * gain_ref[...]).astype(BF16)

    def flat(i):
        return g[i].reshape(tokens, width)

    def section_copy(src):
        return remote(src, hop, hop_send, hop_recv, {"section": 1 - sec})

    @pl.when(sec == 0)
    def _():
        g[0, z, y] = normed_of(x_ref[...].astype(F32))

    @pl.when(sec == 1)
    def _():
        g[0, z, y] = cot_ref[...]

    gather_first(0)

    for m in range(3):
        raw[m][:, slots] = jnp.zeros((hb, block, block), BF16)
    wd[hb * block:] = jnp.zeros((wd.shape[0] - hb * block, width), BF16)
    w_copies[0].wait()
    w_copies[1].wait()

    @pl.loop(0, kb)
    def _(k):
        for m in range(2):
            for c in range(hb):
                slot = inv_ref[(m * hb + c) * kb + k]
                at = (2 * c + m) * block
                wgu[pl.ds(k * block, block), at : at + block] = raw[m][c, slot]

    gather_second(0)
    w_copies[2].wait()

    @pl.loop(0, kb)
    def _(k):
        column = pl.ds(pl.multiple_of(k * block, block), block)
        for c in range(hb):
            slot = inv_ref[(2 * hb + c) * kb + k]
            wd[c * block : (c + 1) * block, column] = raw[2][c, slot]

    gather_end(0)

    def down_grad_input(i):
        @pl.loop(0, wd.shape[0] // (2 * block))
        def _(p):
            at = pl.multiple_of(p * 2 * block, 2 * block)
            dhid[:, pl.ds(at, 2 * block)] = lax.dot_general(
                flat(i), wd[pl.ds(at, 2 * block), :], NT, preferred_element_type=F32
            )

    @pl.when(sec == 1)
    def _():
        down_grad_input(0)
        section_copy(seg_ref).wait_recv()
        g[1, z, y] = normed_of(hop[...].astype(F32))
        gather_first(1)
        gather_second(1)
        gather_end(1)

    @pl.loop(0, hb)
    def _(c):
        both = jnp.dot(
            flat(sec), wgu[:, pl.ds(pl.multiple_of(c * 2 * block, 2 * block), 2 * block)],
            preferred_element_type=F32,
        )
        gu[c] = both
        gate, upper = both[:, :block], both[:, block:]
        hidden = (gate * jax.nn.sigmoid(gate) * upper).astype(BF16)
        hid[:, pl.ds(pl.multiple_of(c * block, block), block)] = hidden

    def transposes():
        @pl.loop(0, kb)
        def _(k):
            column = pl.ds(pl.multiple_of(k * block, block), block)
            xt[k] = g[sec, :, :, :, column].reshape(tokens, block).T

        @pl.loop(0, hb)
        def _(c):
            hid_t[c] = hid[:, pl.ds(pl.multiple_of(c * block, block), block)].T

    def delta_blocks():
        @pl.loop(0, kb)
        def _(k):
            column = pl.ds(pl.multiple_of(k * block, block), block)
            db[k] = g[1 - sec, :, :, :, column].reshape(tokens, block)

    tile = min(512, half)

    def down(use):
        for part_of in (0, 1):
            @pl.loop(0, half // tile)
            def _(n):
                at = pl.multiple_of(part_of * half + n * tile, tile)
                out = jnp.dot(hid[...], wd[: hb * block, pl.ds(at, tile)], preferred_element_type=F32)
                part[:, :, :, pl.ds(at, tile)] = out.astype(BF16).reshape(side, side, rows, tile)
            scatter_start(use, part_of)

    def back(use):
        for part_of in (0, 1):
            @pl.loop(0, half // tile)
            def _(n):
                at = pl.multiple_of(part_of * half + n * tile, tile)
                out = lax.dot_general(
                    dgu[...], wgu[pl.ds(at, tile), :], NT, preferred_element_type=F32
                )
                part[:, :, :, pl.ds(at, tile)] = out.astype(BF16).reshape(side, side, rows, tile)
            scatter_start(use, part_of)

    def input_grad(values, delta, d_norm):
        scale = scale_of(values)
        scaled = gain_ref[...] * d_norm
        spread = jnp.mean(scaled * values, axis=-1, keepdims=True)
        return (delta + scale * scaled - values * (scale * scale * scale) * spread).astype(BF16)

    @pl.when(sec == 0)
    def _():
        down(0)
        scatter_middle(0)
        seg_ref[...] = (x_ref[...].astype(F32) + scatter_end(0)).astype(BF16)
        sent = section_copy(seg_ref)
        sent.start()
        transposes()
        sent.wait_send()
        sent.wait_recv()
        g[1, z, y] = hop[...]
        gather_first(1)
        gather_second(1)
        gather_end(1)
        down_grad_input(1)

    @pl.loop(0, hb)
    def _(c):
        gate, upper = gu[c, :, :block], gu[c, :, block:]
        d_hidden = dhid[:, pl.ds(pl.multiple_of(c * block, block), block)]
        sig = jax.nn.sigmoid(gate)
        d_gate = d_hidden * upper * sig * (1.0 + gate * (1.0 - sig))
        d_up = d_hidden * gate * sig
        at = pl.multiple_of(c * 2 * block, 2 * block)
        dgu[:, pl.ds(at, block)] = d_gate.astype(BF16)
        dgu[:, pl.ds(pl.multiple_of(at + block, block), block)] = d_up.astype(BF16)

    @pl.when(sec == 1)
    def _():
        back(0)
        transposes()
        scatter_middle(0)
        ing_ref[...] = input_grad(hop[...].astype(F32), cot_ref[...].astype(F32), scatter_end(0))
        section_copy(ing_ref).start()

    delta_blocks()
    first, second = slice(0, slots // 2), slice(slots // 2, slots)

    def quarter_of(q):
        return pl.ds(pl.multiple_of(q * quarter, quarter), quarter)

    def ring_first(m, c):
        i = m * hb + c
        q = quarter_of(across)
        return (
            remote(raw[m].at[c, first, q], ex1.at[0, m, c], ex_send.at[0, 0, i], ex_recv.at[0, 0, i], {"dp": right}),
            remote(raw[m].at[c, second, q], ex1.at[1, m, c], ex_send.at[0, 1, i], ex_recv.at[0, 1, i], {"dp": left}),
        )

    def ring_second(m, c):
        i = m * hb + c
        here = pl.ds(0, slots)
        return (
            remote(raw[m].at[c, here, quarter_of(right)], ex2.at[0, m, c], ex_send.at[1, 0, i], ex_recv.at[1, 0, i], {"dp": right}),
            remote(raw[m].at[c, here, quarter_of(left)], ex2.at[1, m, c], ex_send.at[1, 1, i], ex_recv.at[1, 1, i], {"dp": left}),
        )

    def pass_on(m, c):
        for copy, into, which, arrived in zip(ring_first(m, c), (right, left), (first, second), (0, 1)):
            copy.wait_recv()
            q = quarter_of(into)
            mine = raw[m][c, which, q, :].astype(F32)
            raw[m][c, which, q, :] = (mine + ex1[arrived, m, c].astype(F32)).astype(BF16)
        for copy in ring_second(m, c):
            copy.start()

    def live_of(m, c, j):
        return live_ref[(m * hb + c) * slots + j].astype(F32)

    @pl.loop(0, hb)
    def _(c):
        picked = []
        for j in range(slots):
            picked.append(db[rows_ref[(2 * hb + c) * slots + j]])
        out = jnp.dot(hid_t[c], jnp.concatenate(picked, axis=1), preferred_element_type=F32)
        for j in range(slots):
            raw[2][c, j] = (out[:, j * block : (j + 1) * block] * live_of(2, c, j)).astype(BF16)
        for copy in ring_first(2, c):
            copy.start()

    for m in range(2):
        @pl.loop(0, hb)
        def _(c):
            at = pl.multiple_of((2 * c + m) * block, block)
            d_block = dgu[:, pl.ds(at, block)]
            picked = [xt[rows_ref[(m * hb + c) * slots + j]] for j in range(slots)]
            out = jnp.dot(jnp.concatenate(picked, axis=0), d_block, preferred_element_type=F32)
            for j in range(slots):
                raw[m][c, j] = (out[j * block : (j + 1) * block] * live_of(m, c, j)).astype(BF16)
            for copy in ring_first(m, c):
                copy.start()
            pass_on((m + 2) % 3, c)

    @pl.loop(0, hb)
    def _(c):
        pass_on(1, c)

    @pl.when(sec == 0)
    def _():
        back(1)
        scatter_middle(1)
        ing_ref[...] = input_grad(x_ref[...].astype(F32), hop[...].astype(F32), scatter_end(1))

    @pl.when(sec == 1)
    def _():
        section_copy(ing_ref).wait_send()
        down(1)
        scatter_middle(1)
        seg_ref[...] = (hop[...].astype(F32) + scatter_end(1)).astype(BF16)

    for m in (2, 0, 1):
        @pl.loop(0, hb)
        def _(c):
            for copy in ring_second(m, c):
                copy.wait_recv()
            total = raw[m][c, pl.ds(0, slots), quarter_of(me), :].astype(F32)
            for way in (0, 1):
                total = total + ex2[way, m, c].astype(F32)
            wg_ref[m, c] = total.astype(BF16)
            for copy in ring_first(m, c) + ring_second(m, c):
                copy.wait_send()


def shards(inputs, cotangent, gains, weights, block_rows, block_count):
    n_dp, n_ts = lax.axis_size("dp"), lax.axis_size("ts")
    side = math.isqrt(n_ts)
    micro, shard_rows, width = inputs.shape
    rows = micro * shard_rows
    _, _, hb, slots, block, _ = weights.shape
    kb = width // block
    half = width // 2
    quarter = block // n_dp
    tokens = rows * n_ts
    lists = block_rows[0]
    live = jnp.arange(slots)[None, None, :] < block_count[0][:, :, None]
    match = (lists[..., None] == jnp.arange(kb)) & live[..., None]
    inverse = jnp.min(jnp.where(match, jnp.arange(slots)[:, None], slots), axis=2)
    vmem = pl.BlockSpec(memory_space=pltpu.VMEM)
    smem = pl.BlockSpec(memory_space=pltpu.SMEM)
    hb2 = (hb + 1) // 2 * 2
    seg, ing, wg = pl.pallas_call(
        functools.partial(kernel, side, n_dp),
        out_shape=(
            jax.ShapeDtypeStruct((rows, width), BF16),
            jax.ShapeDtypeStruct((rows, width), BF16),
            jax.ShapeDtypeStruct((3, hb, slots, quarter, block), BF16),
        ),
        in_specs=[vmem, vmem, vmem, pl.BlockSpec(memory_space=pl.ANY), smem, smem, smem],
        out_specs=(vmem, vmem, vmem),
        scratch_shapes=[
            pltpu.VMEM((hb, slots + 1, block, block), BF16),
            pltpu.VMEM((hb, slots + 1, block, block), BF16),
            pltpu.VMEM((hb, slots + 1, block, block), BF16),
            pltpu.VMEM((width, 2 * hb * block), BF16),
            pltpu.VMEM((hb2 * block, width), BF16),
            pltpu.VMEM((2, side, side, rows, width), BF16),
            pltpu.VMEM((side, side, rows, width), BF16),
            pltpu.VMEM((2, 2, side - 1, side, rows, half), BF16),
            pltpu.VMEM((2, 2, side - 1, rows, half), BF16),
            pltpu.VMEM((2, side, rows, half), BF16),
            pltpu.VMEM((rows, width), BF16),
            pltpu.VMEM((hb, tokens, 2 * block), F32),
            pltpu.VMEM((tokens, hb2 * block), F32),
            pltpu.VMEM((tokens, hb * block), BF16),
            pltpu.VMEM((hb, block, tokens), BF16),
            pltpu.VMEM((tokens, 2 * hb * block), BF16),
            pltpu.VMEM((kb, block, tokens), BF16),
            pltpu.VMEM((kb, tokens, block), BF16),
            pltpu.VMEM((2, 3, hb, slots // 2, quarter, block), BF16),
            pltpu.VMEM((2, 3, hb, slots, quarter, block), BF16),
            pltpu.SemaphoreType.DMA((3,)),
            pltpu.SemaphoreType.DMA((2, 4, side - 1)),
            pltpu.SemaphoreType.DMA((2, 4, side - 1)),
            pltpu.SemaphoreType.DMA((2, 4, side - 1)),
            pltpu.SemaphoreType.DMA((2, 4, side - 1)),
            pltpu.SemaphoreType.DMA,
            pltpu.SemaphoreType.DMA,
            pltpu.SemaphoreType.DMA((2, 2, 3 * hb)),
            pltpu.SemaphoreType.DMA((2, 2, 3 * hb)),
        ],
        compiler_params=pltpu.CompilerParams(
            collective_id=0, has_side_effects=True, vmem_limit_bytes=63 * 1024 * 1024
        ),
    )(
        inputs.reshape(rows, width),
        cotangent.reshape(rows, width),
        gains,
        weights[0],
        inverse.reshape(-1).astype(jnp.int32),
        lists.reshape(-1),
        live.reshape(-1).astype(jnp.int32),
    )
    shape = (1, micro, shard_rows, width)
    return seg.reshape(shape), ing.reshape(shape), wg[None]


def solution(mesh):
    in_specs = (
        P(None, ("dp", "ts"), None),
        P(None, ("dp", "ts"), None),
        P("section", None),
        P("section", None, "ts", None, None, None),
        P("section", None, "ts", None),
        P("section", None, "ts"),
    )
    out_specs = (
        P("section", None, ("dp", "ts"), None),
        P("section", None, ("dp", "ts"), None),
        P("section", None, "ts", None, "dp", None),
    )
    return jax.shard_map(shards, mesh=mesh, in_specs=in_specs, out_specs=out_specs, check_vma=False)
```

```python
import functools
import math

import jax
import jax.numpy as jnp
from jax import lax
from jax.experimental import pallas as pl
from jax.experimental.pallas import tpu as pltpu
from jax.sharding import PartitionSpec as P

EPSILON = 1e-05
MESH = pl.DeviceIdType.MESH
F32 = jnp.float32
BF16 = jnp.bfloat16
NT = (((1,), (1,)), ((), ()))


def kernel(
    side, n_dp,
    x_ref, cot_ref, gain_ref, w_hbm, inv_ref, rows_ref, live_ref,
    seg_ref, ing_ref, wg_ref,
    raw0, raw1, raw2, wgu, wd, g, part, rs1, rs2, mid, hop, stage, gain_x, gu, dhid, hid, hid_t, dgu, xt, db, ex1, ex2,
    w_sem, ag_send, ag_recv, rs_send, rs_recv, hop_send, hop_recv, ex_send, ex_recv,
):
    rows, width = x_ref.shape
    chunk = width // 4
    _, hb, slots, block, _ = w_hbm.shape
    kb = width // block
    tokens = side * side * rows
    quarter = block // n_dp
    sec = lax.axis_index("section")
    ts = lax.axis_index("ts")
    me = lax.axis_index("dp")
    z, y = ts // side, lax.rem(ts, side)
    right, left = lax.rem(me + 1, n_dp), lax.rem(me + n_dp - 1, n_dp)
    across = lax.rem(me + 2, n_dp)
    raw = (raw0, raw1, raw2)
    cols = [slice(q * chunk, (q + 1) * chunk) for q in range(4)]
    order = (0, 2, 1, 3)
    peers = [(lax.rem(z + d, side), lax.rem(y + d, side)) for d in range(side)]
    others = range(1, side)

    w_copies = [
        pltpu.make_async_copy(w_hbm.at[m], raw[m].at[:, pl.ds(0, slots)], w_sem.at[m])
        for m in range(3)
    ]
    for copy in w_copies:
        copy.start()

    barrier = pltpu.get_barrier_semaphore()

    def greet(where):
        pl.semaphore_signal(barrier, inc=1, device_id=where, device_id_type=MESH)

    for d in others:
        pz, py = peers[d]
        for s in (0, 1):
            greet({"ts": pz * side + y, "section": s})
            greet({"ts": z * side + py, "section": s})
    greet({"dp": right})
    greet({"dp": left})
    greet({"section": 1 - sec})

    def remote(src, dst, send, recv, where):
        return pltpu.make_async_remote_copy(
            src_ref=src, dst_ref=dst, send_sem=send, recv_sem=recv,
            device_id=where, device_id_type=MESH,
        )

    def gather_copies(i, phase, q, src=None):
        first = q < 2
        along_y = first == (phase == 0)
        copies = []
        for d in range(side):
            pz, py = peers[d]
            where = {"ts": z * side + py} if along_y else {"ts": pz * side + y}
            if phase == 0:
                dst = g.at[i, z, y, :, cols[q]]
                ref = dst
                if i == 1:
                    ref = src.at[:, cols[q]]
                    where["section"] = 1 - sec
                elif d == 0:
                    continue
            else:
                if d == 0:
                    continue
                ref = g.at[i, z, :, :, cols[q]] if first else g.at[i, :, y, :, cols[q]]
                dst = ref
            copies.append(remote(ref, dst, ag_send.at[i, phase, q, d], ag_recv.at[i, phase, q, d], where))
        return copies

    def gather_first(i, src=None):
        for q in order:
            for copy in gather_copies(i, 0, q, src):
                copy.start()

    def gather_second(i):
        for q in order:
            for copy in gather_copies(i, 0, q, stage):
                copy.wait_recv()
            for copy in gather_copies(i, 1, q):
                copy.start()

    def gather_end(i, q):
        for copy in gather_copies(i, 1, q):
            copy.wait_recv()

    def scatter_copies(use, phase, q):
        first = q < 2
        along_y = first == (phase == 1)
        copies = []
        for d in others:
            pz, py = peers[d]
            where = {"ts": z * side + py} if along_y else {"ts": pz * side + y}
            if phase == 0:
                src = part.at[pz, :, :, cols[q]] if first else part.at[:, py, :, cols[q]]
                dst = rs1.at[use, q, d - 1]
            else:
                src = mid.at[q, py if first else pz]
                dst = rs2.at[use, q, d - 1]
            copies.append(
                remote(src, dst, rs_send.at[use, phase, q, d - 1], rs_recv.at[use, phase, q, d - 1], where)
            )
        return copies

    def scatter_start(use, q):
        for copy in scatter_copies(use, 0, q):
            copy.start()

    def scatter_middle(use):
        for q in order:
            for copy in scatter_copies(use, 0, q):
                copy.wait_recv()
            for i in range(side):
                own = part[z, i, :, cols[q]] if q < 2 else part[i, y, :, cols[q]]
                total = own.astype(F32)
                for d in range(side - 1):
                    total = total + rs1[use, q, d, i].astype(F32)
                mid[q, i] = total.astype(BF16)
            for copy in scatter_copies(use, 1, q):
                copy.start()

    def scatter_end(use):
        totals = []
        for q in range(4):
            for copy in scatter_copies(use, 1, q):
                copy.wait_recv()
            total = mid[q, y if q < 2 else z].astype(F32)
            for d in range(side - 1):
                total = total + rs2[use, q, d].astype(F32)
            totals.append(total)
        return jnp.concatenate(totals, axis=1)

    def scatter_sent(use):
        for phase in (0, 1):
            for q in range(4):
                for copy in scatter_copies(use, phase, q):
                    copy.wait_send()

    def scale_of(values):
        return lax.rsqrt(jnp.mean(values * values, axis=-1, keepdims=True) + EPSILON)

    def normed_of(values, gain):
        return (values * scale_of(values) * gain).astype(BF16)

    def wide(i, q):
        return g[i, :, :, :, cols[q]].reshape(tokens, chunk)

    def act_copy():
        return remote(seg_ref, hop, hop_send.at[0], hop_recv.at[0], {"section": 1})

    def gain_copy():
        return remote(gain_ref, gain_x, hop_send.at[1], hop_recv.at[1], {"section": 0})

    @pl.when(sec == 0)
    def _():
        g[0, z, y] = normed_of(x_ref[...].astype(F32), gain_ref[...])

    @pl.when(sec == 1)
    def _():
        g[0, z, y] = cot_ref[...]

    pl.semaphore_wait(barrier, 4 * (side - 1) + 3)
    gather_first(0)

    @pl.when(sec == 1)
    def _():
        gain_copy().start()

    for m in range(3):
        raw[m][:, slots] = jnp.zeros((hb, block, block), BF16)
    w_copies[0].wait()
    w_copies[1].wait()

    @pl.loop(0, kb)
    def _(k):
        for m in range(2):
            for c in range(hb):
                slot = inv_ref[(m * hb + c) * kb + k]
                at = (2 * c + m) * block
                wgu[pl.ds(k * block, block), at : at + block] = raw[m][c, slot]

    gather_second(0)
    w_copies[2].wait()

    @pl.loop(0, kb)
    def _(k):
        column = pl.ds(pl.multiple_of(k * block, block), block)
        for c in range(hb):
            slot = inv_ref[(2 * hb + c) * kb + k]
            wd[c * block : (c + 1) * block, column] = raw[2][c, slot]

    per_chunk = chunk // block

    def transposed(i, q):
        @pl.loop(0, per_chunk)
        def _(k):
            column = pl.ds(pl.multiple_of(q * chunk + k * block, block), block)
            xt[q * per_chunk + k] = g[i, :, :, :, column].reshape(tokens, block).T

    def delta_blocks(i, q):
        @pl.loop(0, per_chunk)
        def _(k):
            column = pl.ds(pl.multiple_of(q * chunk + k * block, block), block)
            db[q * per_chunk + k] = g[i, :, :, :, column].reshape(tokens, block)

    def down_grad_input(i):
        for n, q in enumerate(order):
            gather_end(i, q)
            term = lax.dot_general(wide(i, q), wd[:, cols[q]], NT, preferred_element_type=F32)
            dhid[...] = term if n == 0 else dhid[...] + term
            delta_blocks(i, q)

    def gate_and_up(i):
        for n, q in enumerate(order):
            gather_end(i, q)
            term = jnp.dot(wide(i, q), wgu[cols[q], :], preferred_element_type=F32)
            gu[...] = term if n == 0 else gu[...] + term
            if n < 3:
                transposed(i, q)

    @pl.when(sec == 0)
    def _():
        gate_and_up(0)

    @pl.when(sec == 1)
    def _():
        down_grad_input(0)
        gather_second(1)
        gate_and_up(1)

    def gate_of(c):
        at = pl.multiple_of(c * 2 * block, 2 * block)
        return gu[:, pl.ds(at, block)], gu[:, pl.ds(pl.multiple_of(at + block, block), block)]

    @pl.loop(0, hb)
    def _(c):
        gate, upper = gate_of(c)
        hid[:, pl.ds(pl.multiple_of(c * block, block), block)] = (
            gate * jax.nn.sigmoid(gate) * upper
        ).astype(BF16)

    def hidden_transposed():
        transposed(sec, order[3])

        @pl.loop(0, hb)
        def _(c):
            hid_t[c] = hid[:, pl.ds(pl.multiple_of(c * block, block), block)].T

    def down(use):
        for q in order:
            out = jnp.dot(hid[...], wd[:, cols[q]], preferred_element_type=F32)
            part[:, :, :, cols[q]] = out.astype(BF16).reshape(side, side, rows, chunk)
            scatter_start(use, q)

    def back(use):
        for q in order:
            out = lax.dot_general(dgu[...], wgu[cols[q], :], NT, preferred_element_type=F32)
            part[:, :, :, cols[q]] = out.astype(BF16).reshape(side, side, rows, chunk)
            scatter_start(use, q)

    def input_grad(values, delta, d_norm):
        scale = scale_of(values)
        scaled = gain_ref[...] * d_norm
        spread = jnp.mean(scaled * values, axis=-1, keepdims=True)
        return (delta + scale * scaled - values * (scale * scale * scale) * spread).astype(BF16)

    def pre_activation_grads():
        @pl.loop(0, hb)
        def _(c):
            gate, upper = gate_of(c)
            d_hidden = dhid[:, pl.ds(pl.multiple_of(c * block, block), block)]
            sig = jax.nn.sigmoid(gate)
            d_gate = d_hidden * upper * sig * (1.0 + gate * (1.0 - sig))
            d_up = d_hidden * gate * sig
            at = pl.multiple_of(c * 2 * block, 2 * block)
            dgu[:, pl.ds(at, block)] = d_gate.astype(BF16)
            dgu[:, pl.ds(pl.multiple_of(at + block, block), block)] = d_up.astype(BF16)

    first, second = slice(0, slots // 2), slice(slots // 2, slots)

    def quarter_of(q):
        return pl.ds(pl.multiple_of(q * quarter, quarter), quarter)

    def ring_first(m, c):
        i = m * hb + c
        q = quarter_of(across)
        return (
            remote(raw[m].at[c, first, q], ex1.at[0, m, c], ex_send.at[0, 0, i], ex_recv.at[0, 0, i], {"dp": right}),
            remote(raw[m].at[c, second, q], ex1.at[1, m, c], ex_send.at[0, 1, i], ex_recv.at[0, 1, i], {"dp": left}),
        )

    def ring_second(m, c):
        i = m * hb + c
        here = pl.ds(0, slots)
        return (
            remote(raw[m].at[c, here, quarter_of(right)], ex2.at[0, m, c], ex_send.at[1, 0, i], ex_recv.at[1, 0, i], {"dp": right}),
            remote(raw[m].at[c, here, quarter_of(left)], ex2.at[1, m, c], ex_send.at[1, 1, i], ex_recv.at[1, 1, i], {"dp": left}),
        )

    def pass_on(m):
        @pl.loop(0, hb)
        def _(c):
            for copy, into, which, arrived in zip(ring_first(m, c), (right, left), (first, second), (0, 1)):
                copy.wait_recv()
                q = quarter_of(into)
                mine = raw[m][c, which, q, :].astype(F32)
                raw[m][c, which, q, :] = (mine + ex1[arrived, m, c].astype(F32)).astype(BF16)
            for copy in ring_second(m, c):
                copy.start()

    def live_of(m, c, j):
        return live_ref[(m * hb + c) * slots + j].astype(F32)

    def down_weight_grads():
        @pl.loop(0, hb)
        def _(c):
            picked = [db[rows_ref[(2 * hb + c) * slots + j]] for j in range(slots)]
            out = jnp.dot(hid_t[c], jnp.concatenate(picked, axis=1), preferred_element_type=F32)
            for j in range(slots):
                raw[2][c, j] = (out[:, j * block : (j + 1) * block] * live_of(2, c, j)).astype(BF16)
            for copy in ring_first(2, c):
                copy.start()

    def weight_grads(m):
        @pl.loop(0, hb)
        def _(c):
            at = pl.multiple_of((2 * c + m) * block, block)
            d_block = dgu[:, pl.ds(at, block)]
            picked = [xt[rows_ref[(m * hb + c) * slots + j]] for j in range(slots)]
            out = jnp.dot(jnp.concatenate(picked, axis=0), d_block, preferred_element_type=F32)
            for j in range(slots):
                raw[m][c, j] = (out[j * block : (j + 1) * block] * live_of(m, c, j)).astype(BF16)
            for copy in ring_first(m, c):
                copy.start()

    @pl.when(sec == 0)
    def _():
        down(0)
        hidden_transposed()
        gain_copy().wait_recv()
        scatter_middle(0)
        act = (x_ref[...].astype(F32) + scatter_end(0)).astype(BF16)
        seg_ref[...] = act
        stage[...] = normed_of(act.astype(F32), gain_x[...])
        gather_first(1, stage)
        act_copy().start()
        scatter_sent(0)
        gather_second(1)
        down_grad_input(1)
        down_weight_grads()
        pre_activation_grads()
        weight_grads(0)
        weight_grads(1)
        pass_on(2)
        back(1)
        pass_on(0)
        scatter_middle(1)
        pass_on(1)
        ing_ref[...] = input_grad(x_ref[...].astype(F32), g[1, z, y].astype(F32), scatter_end(1))
        act_copy().wait_send()

    @pl.when(sec == 1)
    def _():
        pre_activation_grads()
        back(0)
        hidden_transposed()
        down_weight_grads()
        weight_grads(0)
        act_copy().wait_recv()
        scatter_middle(0)
        weight_grads(1)
        ing_ref[...] = input_grad(hop[...].astype(F32), cot_ref[...].astype(F32), scatter_end(0))
        stage[...] = ing_ref[...]
        gather_first(1, stage)
        scatter_sent(0)
        pass_on(2)
        pass_on(0)
        down(1)
        pass_on(1)
        scatter_middle(1)
        seg_ref[...] = (hop[...].astype(F32) + scatter_end(1)).astype(BF16)
        gain_copy().wait_send()

    for m in (2, 0, 1):
        @pl.loop(0, hb)
        def _(c):
            for copy in ring_second(m, c):
                copy.wait_recv()
            total = raw[m][c, pl.ds(0, slots), quarter_of(me), :].astype(F32)
            for way in (0, 1):
                total = total + ex2[way, m, c].astype(F32)
            wg_ref[m, c] = total.astype(BF16)

    scatter_sent(1)
    for i in (0, 1):
        for phase in (0, 1):
            for q in range(4):
                for copy in gather_copies(i, phase, q, stage):
                    copy.wait_send()
    for m in range(3):
        @pl.loop(0, hb)
        def _(c):
            for copy in ring_first(m, c) + ring_second(m, c):
                copy.wait_send()


def shards(inputs, cotangent, gains, weights, block_rows, block_count):
    n_dp, n_ts = lax.axis_size("dp"), lax.axis_size("ts")
    side = math.isqrt(n_ts)
    micro, shard_rows, width = inputs.shape
    rows = micro * shard_rows
    _, _, hb, slots, block, _ = weights.shape
    kb = width // block
    chunk = width // 4
    quarter = block // n_dp
    tokens = rows * n_ts
    lists = block_rows[0]
    live = jnp.arange(slots)[None, None, :] < block_count[0][:, :, None]
    match = (lists[..., None] == jnp.arange(kb)) & live[..., None]
    inverse = jnp.min(jnp.where(match, jnp.arange(slots)[:, None], slots), axis=2)
    vmem = pl.BlockSpec(memory_space=pltpu.VMEM)
    smem = pl.BlockSpec(memory_space=pltpu.SMEM)
    seg, ing, wg = pl.pallas_call(
        functools.partial(kernel, side, n_dp),
        out_shape=(
            jax.ShapeDtypeStruct((rows, width), BF16),
            jax.ShapeDtypeStruct((rows, width), BF16),
            jax.ShapeDtypeStruct((3, hb, slots, quarter, block), BF16),
        ),
        in_specs=[vmem, vmem, vmem, pl.BlockSpec(memory_space=pl.ANY), smem, smem, smem],
        out_specs=(vmem, vmem, vmem),
        scratch_shapes=[
            pltpu.VMEM((hb, slots + 1, block, block), BF16),
            pltpu.VMEM((hb, slots + 1, block, block), BF16),
            pltpu.VMEM((hb, slots + 1, block, block), BF16),
            pltpu.VMEM((width, 2 * hb * block), BF16),
            pltpu.VMEM((hb * block, width), BF16),
            pltpu.VMEM((2, side, side, rows, width), BF16),
            pltpu.VMEM((side, side, rows, width), BF16),
            pltpu.VMEM((2, 4, side - 1, side, rows, chunk), BF16),
            pltpu.VMEM((2, 4, side - 1, rows, chunk), BF16),
            pltpu.VMEM((4, side, rows, chunk), BF16),
            pltpu.VMEM((rows, width), BF16),
            pltpu.VMEM((rows, width), BF16),
            pltpu.VMEM((1, width), F32),
            pltpu.VMEM((tokens, 2 * hb * block), F32),
            pltpu.VMEM((tokens, hb * block), F32),
            pltpu.VMEM((tokens, hb * block), BF16),
            pltpu.VMEM((hb, block, tokens), BF16),
            pltpu.VMEM((tokens, 2 * hb * block), BF16),
            pltpu.VMEM((kb, block, tokens), BF16),
            pltpu.VMEM((kb, tokens, block), BF16),
            pltpu.VMEM((2, 3, hb, slots // 2, quarter, block), BF16),
            pltpu.VMEM((2, 3, hb, slots, quarter, block), BF16),
            pltpu.SemaphoreType.DMA((3,)),
            pltpu.SemaphoreType.DMA((2, 2, 4, side)),
            pltpu.SemaphoreType.DMA((2, 2, 4, side)),
            pltpu.SemaphoreType.DMA((2, 2, 4, side - 1)),
            pltpu.SemaphoreType.DMA((2, 2, 4, side - 1)),
            pltpu.SemaphoreType.DMA((2,)),
            pltpu.SemaphoreType.DMA((2,)),
            pltpu.SemaphoreType.DMA((2, 2, 3 * hb)),
            pltpu.SemaphoreType.DMA((2, 2, 3 * hb)),
        ],
        compiler_params=pltpu.CompilerParams(
            collective_id=0, has_side_effects=True, vmem_limit_bytes=63 * 1024 * 1024
        ),
    )(
        inputs.reshape(rows, width),
        cotangent.reshape(rows, width),
        gains,
        weights[0],
        inverse.reshape(-1).astype(jnp.int32),
        lists.reshape(-1),
        live.reshape(-1).astype(jnp.int32),
    )
    shape = (1, micro, shard_rows, width)
    return seg.reshape(shape), ing.reshape(shape), wg[None]


def solution(mesh):
    in_specs = (
        P(None, ("dp", "ts"), None),
        P(None, ("dp", "ts"), None),
        P("section", None),
        P("section", None, "ts", None, None, None),
        P("section", None, "ts", None),
        P("section", None, "ts"),
    )
    out_specs = (
        P("section", None, ("dp", "ts"), None),
        P("section", None, ("dp", "ts"), None),
        P("section", None, "ts", None, "dp", None),
    )
    return jax.shard_map(shards, mesh=mesh, in_specs=in_specs, out_specs=out_specs, check_vma=False)
```

```python
import functools
import math

import jax
import jax.numpy as jnp
from jax import lax
from jax.experimental import pallas as pl
from jax.experimental.pallas import tpu as pltpu
from jax.sharding import PartitionSpec as P

EPSILON = 1e-05
MESH = pl.DeviceIdType.MESH
F32 = jnp.float32
BF16 = jnp.bfloat16
NT = (((1,), (1,)), ((), ()))


def kernel(
    side, n_dp,
    x_ref, cot_ref, gain_ref, w_hbm, rows_ref, count_ref,
    seg_ref, ing_ref, wg_ref,
    raw0, raw1, raw2, wgu, wd, g, part, rs1, rs2, mid, hop, stage, gain_x, gu, dhid, hid, hid_t, dgu, da, xt, xa, db, ex1, ex2,
    w_sem, ag_send, ag_recv, rs_send, rs_recv, hop_send, hop_recv, ex_send, ex_recv,
    da_send, da_recv, xa_send, xa_recv, go, inv_v, inv, inv_sem,
):
    rows, width = x_ref.shape
    chunk = width // 4
    _, hb, slots, block, _ = w_hbm.shape
    kb = width // block
    tokens = side * side * rows
    quarter = block // n_dp
    sec = lax.axis_index("section")
    ts = lax.axis_index("ts")
    me = lax.axis_index("dp")
    z, y = ts // side, lax.rem(ts, side)
    right, left = lax.rem(me + 1, n_dp), lax.rem(me + n_dp - 1, n_dp)
    across = lax.rem(me + 2, n_dp)
    raw = (raw0, raw1, raw2)
    cols = [slice(q * chunk, (q + 1) * chunk) for q in range(4)]
    order = (0, 2, 1, 3)
    peers = [(lax.rem(z + d, side), lax.rem(y + d, side)) for d in range(side)]
    others = range(1, side)

    w_copies = [
        pltpu.make_async_copy(w_hbm.at[m], raw[m].at[:, pl.ds(0, slots)], w_sem.at[m])
        for m in range(3)
    ]
    for copy in w_copies:
        copy.start()

    barrier = pltpu.get_barrier_semaphore()

    def greet(where):
        pl.semaphore_signal(barrier, inc=1, device_id=where, device_id_type=MESH)

    for d in others:
        pz, py = peers[d]
        for s in (0, 1):
            greet({"ts": pz * side + y, "section": s})
            greet({"ts": z * side + py, "section": s})
    for other in (right, left, across):
        greet({"dp": other})
    greet({"section": 1 - sec})

    def remote(src, dst, send, recv, where):
        return pltpu.make_async_remote_copy(
            src_ref=src, dst_ref=dst, send_sem=send, recv_sem=recv,
            device_id=where, device_id_type=MESH,
        )

    def gather_copies(i, phase, q, src=None):
        first = q < 2
        along_y = first == (phase == 0)
        copies = []
        for d in range(side):
            pz, py = peers[d]
            where = {"ts": z * side + py} if along_y else {"ts": pz * side + y}
            if phase == 0:
                dst = g.at[i, z, y, :, cols[q]]
                ref = dst
                if i == 1:
                    ref = src.at[:, cols[q]]
                    where["section"] = 1 - sec
                elif d == 0:
                    continue
            else:
                if d == 0:
                    continue
                ref = g.at[i, z, :, :, cols[q]] if first else g.at[i, :, y, :, cols[q]]
                dst = ref
            copies.append(remote(ref, dst, ag_send.at[i, phase, q, d], ag_recv.at[i, phase, q, d], where))
        return copies

    def gather_first(i, src=None):
        for q in order:
            for copy in gather_copies(i, 0, q, src):
                copy.start()

    def gather_second(i, some=order):
        for q in some:
            for copy in gather_copies(i, 0, q, stage):
                copy.wait_recv()
            for copy in gather_copies(i, 1, q):
                copy.start()

    def gather_end(i, q):
        for copy in gather_copies(i, 1, q):
            copy.wait_recv()

    def scatter_copies(use, phase, q):
        first = q < 2
        along_y = first == (phase == 1)
        copies = []
        for d in others:
            pz, py = peers[d]
            where = {"ts": z * side + py} if along_y else {"ts": pz * side + y}
            if phase == 0:
                src = part.at[pz, :, :, cols[q]] if first else part.at[:, py, :, cols[q]]
                dst = rs1.at[use, q, d - 1]
            else:
                src = mid.at[q, py if first else pz]
                dst = rs2.at[use, q, d - 1]
            copies.append(
                remote(src, dst, rs_send.at[use, phase, q, d - 1], rs_recv.at[use, phase, q, d - 1], where)
            )
        return copies

    def scatter_start(use, q):
        for copy in scatter_copies(use, 0, q):
            copy.start()

    def scatter_middle(use):
        for q in order:
            for copy in scatter_copies(use, 0, q):
                copy.wait_recv()
            for i in range(side):
                own = part[z, i, :, cols[q]] if q < 2 else part[i, y, :, cols[q]]
                total = own.astype(F32)
                for d in range(side - 1):
                    total = total + rs1[use, q, d, i].astype(F32)
                mid[q, i] = total.astype(BF16)
            for copy in scatter_copies(use, 1, q):
                copy.start()

    def scatter_end(use):
        totals = []
        for q in range(4):
            for copy in scatter_copies(use, 1, q):
                copy.wait_recv()
            total = mid[q, y if q < 2 else z].astype(F32)
            for d in range(side - 1):
                total = total + rs2[use, q, d].astype(F32)
            totals.append(total)
        return jnp.concatenate(totals, axis=1)

    def scatter_sent(use):
        for phase in (0, 1):
            for q in range(4):
                for copy in scatter_copies(use, phase, q):
                    copy.wait_send()

    def scale_of(values):
        return lax.rsqrt(jnp.mean(values * values, axis=-1, keepdims=True) + EPSILON)

    def normed_of(values, gain):
        return (values * scale_of(values) * gain).astype(BF16)

    def wide(i, q):
        return g[i, :, :, :, cols[q]].reshape(tokens, chunk)

    def act_copy():
        return remote(seg_ref, hop, hop_send.at[0], hop_recv.at[0], {"section": 1})

    def gain_copy():
        return remote(gain_ref, gain_x, hop_send.at[1], hop_recv.at[1], {"section": 0})

    @pl.when(sec == 0)
    def _():
        g[0, z, y] = normed_of(x_ref[...].astype(F32), gain_ref[...])

    @pl.when(sec == 1)
    def _():
        g[0, z, y] = cot_ref[...]

    pl.semaphore_wait(barrier, 4 * (side - 1) + 4)
    gather_first(0)

    @pl.when(sec == 1)
    def _():
        gain_copy().start()

    for m in range(3):
        raw[m][:, slots] = jnp.zeros((hb, block, block), BF16)

    lane = lax.broadcasted_iota(jnp.int32, (1, inv_v.shape[1]), 1)
    for m in range(3):
        for c in range(hb):
            found = jnp.full(lane.shape, slots, jnp.int32)
            for j in range(slots):
                row = jnp.where(j < count_ref[m, 0, c], rows_ref[m, c, 0, j], -1)
                found = jnp.where(lane == row, j, found)
            inv_v[pl.ds(m * hb + c, 1), :] = found
    inv_copy = pltpu.make_async_copy(inv_v, inv, inv_sem)
    inv_copy.start()
    inv_copy.wait()
    w_copies[0].wait()
    w_copies[1].wait()

    @pl.loop(0, kb)
    def _(k):
        for m in range(2):
            for c in range(hb):
                slot = inv[m * hb + c, k]
                at = (2 * c + m) * block
                wgu[pl.ds(k * block, block), at : at + block] = raw[m][c, slot]

    @pl.when(sec == 0)
    def _():
        gather_second(0)

    w_copies[2].wait()

    @pl.loop(0, kb)
    def _(k):
        column = pl.ds(pl.multiple_of(k * block, block), block)
        for c in range(hb):
            slot = inv[2 * hb + c, k]
            wd[c * block : (c + 1) * block, column] = raw[2][c, slot]

    per_chunk = chunk // block

    def quarter_of(q):
        return pl.ds(pl.multiple_of(q * quarter, quarter), quarter)

    def normed_copies(q):
        part_of = pl.ds(q * per_chunk, per_chunk)
        return [
            remote(
                xt.at[part_of, quarter_of(to)], xa.at[n + 1, part_of],
                xa_send.at[n, q], xa_recv.at[n, q], {"dp": to},
            )
            for n, to in enumerate((right, left, across))
        ]

    def transposed(i, q):
        @pl.loop(0, per_chunk)
        def _(k):
            column = pl.ds(pl.multiple_of(q * chunk + k * block, block), block)
            xt[q * per_chunk + k] = g[i, :, :, :, column].reshape(tokens, block).T
            xa[0, q * per_chunk + k] = xt[q * per_chunk + k, quarter_of(me), :]

        for copy in normed_copies(q):
            copy.start()

    def delta_blocks(i, q):
        @pl.loop(0, per_chunk)
        def _(k):
            column = pl.ds(pl.multiple_of(q * chunk + k * block, block), block)
            db[q * per_chunk + k] = g[i, :, :, :, column].reshape(tokens, block)

    def down_grad_input(i, some=order):
        for n, q in enumerate(some):
            gather_end(i, q)
            term = lax.dot_general(wide(i, q), wd[:, cols[q]], NT, preferred_element_type=F32)
            dhid[...] = term if q == order[0] else dhid[...] + term
            delta_blocks(i, q)

    def allow(n):
        pl.semaphore_signal(go.at[n], inc=1, device_id={"section": 1}, device_id_type=MESH)

    def gate_and_up(i):
        for n, q in enumerate(order):
            gather_end(i, q)
            term = jnp.dot(wide(i, q), wgu[cols[q], :], preferred_element_type=F32)
            gu[...] = term if n == 0 else gu[...] + term
            if n < 3:
                transposed(i, q)

    @pl.when(sec == 0)
    def _():
        gate_and_up(0)
        allow(0)

    @pl.when(sec == 1)
    def _():
        pl.semaphore_wait(go.at[0], 1)
        gather_second(0, order[:2])
        down_grad_input(0, order[:2])
        pl.semaphore_wait(go.at[1], 1)
        gather_second(0, order[2:])
        down_grad_input(0, order[2:])
        gather_second(1)
        gate_and_up(1)

    def gate_of(c):
        at = pl.multiple_of(c * 2 * block, 2 * block)
        return gu[:, pl.ds(at, block)], gu[:, pl.ds(pl.multiple_of(at + block, block), block)]

    @pl.loop(0, hb)
    def _(c):
        gate, upper = gate_of(c)
        hid[:, pl.ds(pl.multiple_of(c * block, block), block)] = (
            gate * jax.nn.sigmoid(gate) * upper
        ).astype(BF16)

    def hidden_transposed():
        transposed(sec, order[3])

        @pl.loop(0, hb)
        def _(c):
            hid_t[c] = hid[:, pl.ds(pl.multiple_of(c * block, block), block)].T

    def down(use):
        for q in order:
            out = jnp.dot(hid[...], wd[:, cols[q]], preferred_element_type=F32)
            part[:, :, :, cols[q]] = out.astype(BF16).reshape(side, side, rows, chunk)
            scatter_start(use, q)

    def back(use):
        for q in order:
            out = lax.dot_general(dgu[...], wgu[cols[q], :], NT, preferred_element_type=F32)
            part[:, :, :, cols[q]] = out.astype(BF16).reshape(side, side, rows, chunk)
            scatter_start(use, q)

    def input_grad(values, delta, d_norm):
        scale = scale_of(values)
        scaled = gain_ref[...] * d_norm
        spread = jnp.mean(scaled * values, axis=-1, keepdims=True)
        return (delta + scale * scaled - values * (scale * scale * scale) * spread).astype(BF16)

    def pre_activation_grads():
        @pl.loop(0, hb)
        def _(c):
            gate, upper = gate_of(c)
            d_hidden = dhid[:, pl.ds(pl.multiple_of(c * block, block), block)]
            sig = jax.nn.sigmoid(gate)
            d_gate = d_hidden * upper * sig * (1.0 + gate * (1.0 - sig))
            d_up = d_hidden * gate * sig
            at = pl.multiple_of(c * 2 * block, 2 * block)
            dgu[:, pl.ds(at, block)] = d_gate.astype(BF16)
            dgu[:, pl.ds(pl.multiple_of(at + block, block), block)] = d_up.astype(BF16)
            for copy in grad_copies(c, (0, 1)):
                copy.start()

    def grad_copies(c, which=(0, 1, 2, 3)):
        col = pl.ds(pl.multiple_of(c * 2 * block, 2 * block), 2 * block)
        low, high = pl.ds(0, tokens // 2), pl.ds(tokens // 2, tokens // 2)
        moves = (
            (dgu.at[:, col], da.at[0, :, col], right),
            (dgu.at[:, col], da.at[1, :, col], left),
            (da.at[0, low, col], da.at[2, low, col], right),
            (da.at[1, high, col], da.at[2, high, col], left),
        )
        return [
            remote(src, dst, da_send.at[n, c], da_recv.at[n, c], {"dp": to})
            for n, (src, dst, to) in enumerate(moves)
            if n in which
        ]

    def relay():
        @pl.loop(0, hb)
        def _(c):
            for n in (0, 1):
                grad_copies(c, (n,))[0].wait_recv()
                grad_copies(c, (n + 2,))[0].start()

    first, second = slice(0, slots // 2), slice(slots // 2, slots)

    def ring_first(c):
        q = quarter_of(across)
        return (
            remote(raw2.at[c, first, q], ex1.at[0, c], ex_send.at[0, 0, c], ex_recv.at[0, 0, c], {"dp": right}),
            remote(raw2.at[c, second, q], ex1.at[1, c], ex_send.at[0, 1, c], ex_recv.at[0, 1, c], {"dp": left}),
        )

    def ring_second(c):
        here = pl.ds(0, slots)
        return (
            remote(raw2.at[c, here, quarter_of(right)], ex2.at[0, c], ex_send.at[1, 0, c], ex_recv.at[1, 0, c], {"dp": right}),
            remote(raw2.at[c, here, quarter_of(left)], ex2.at[1, c], ex_send.at[1, 1, c], ex_recv.at[1, 1, c], {"dp": left}),
        )

    def pass_on():
        @pl.loop(0, hb)
        def _(c):
            for copy, into, which, arrived in zip(ring_first(c), (right, left), (first, second), (0, 1)):
                copy.wait_recv()
                q = quarter_of(into)
                mine = raw2[c, which, q, :].astype(F32)
                raw2[c, which, q, :] = (mine + ex1[arrived, c].astype(F32)).astype(BF16)
            for copy in ring_second(c):
                copy.start()

    def live_of(m, c, j):
        return (j < count_ref[m, 0, c]).astype(F32)

    def down_weight_grads():
        @pl.loop(0, hb)
        def _(c):
            picked = [db[rows_ref[2, c, 0, j]] for j in range(slots)]
            out = jnp.dot(hid_t[c], jnp.concatenate(picked, axis=1), preferred_element_type=F32)
            for j in range(slots):
                raw2[c, j] = (out[:, j * block : (j + 1) * block] * live_of(2, c, j)).astype(BF16)
            for copy in ring_first(c):
                copy.start()

    def weight_grads():
        for q in range(4):
            for copy in normed_copies(q):
                copy.wait_recv()

        @pl.loop(0, hb)
        def _(c):
            for copy in grad_copies(c, (2, 3)):
                copy.wait_recv()
            for m in range(2):
                col = pl.ds(pl.multiple_of((2 * c + m) * block, block), block)
                grads = jnp.concatenate([dgu[:, col]] + [da[n, :, col] for n in range(3)], axis=0)
                picked = []
                for j in range(slots):
                    row = rows_ref[m, c, 0, j]
                    picked.append(jnp.concatenate([xa[n, row] for n in range(4)], axis=1))
                out = jnp.dot(jnp.concatenate(picked, axis=0), grads, preferred_element_type=F32)
                for j in range(slots):
                    wg_ref[m, c, j] = (out[j * quarter : (j + 1) * quarter] * live_of(m, c, j)).astype(BF16)

    @pl.when(sec == 0)
    def _():
        down(0)
        hidden_transposed()
        gain_copy().wait_recv()
        scatter_middle(0)
        allow(1)
        act = (x_ref[...].astype(F32) + scatter_end(0)).astype(BF16)
        seg_ref[...] = act
        stage[...] = normed_of(act.astype(F32), gain_x[...])
        gather_first(1, stage)
        act_copy().start()
        scatter_sent(0)
        gather_second(1)
        down_grad_input(1)
        allow(2)
        pre_activation_grads()
        down_weight_grads()
        back(1)
        relay()
        pass_on()
        scatter_middle(1)
        weight_grads()
        ing_ref[...] = input_grad(x_ref[...].astype(F32), g[1, z, y].astype(F32), scatter_end(1))
        act_copy().wait_send()

    @pl.when(sec == 1)
    def _():
        pre_activation_grads()
        back(0)
        hidden_transposed()
        down_weight_grads()
        act_copy().wait_recv()
        scatter_middle(0)
        relay()
        ing_ref[...] = input_grad(hop[...].astype(F32), cot_ref[...].astype(F32), scatter_end(0))
        stage[...] = ing_ref[...]
        gather_first(1, stage)
        scatter_sent(0)
        pass_on()
        weight_grads()
        pl.semaphore_wait(go.at[2], 1)
        down(1)
        scatter_middle(1)
        seg_ref[...] = (hop[...].astype(F32) + scatter_end(1)).astype(BF16)
        gain_copy().wait_send()

    @pl.loop(0, hb)
    def _(c):
        for copy in ring_second(c):
            copy.wait_recv()
        total = raw2[c, pl.ds(0, slots), quarter_of(me), :].astype(F32)
        for way in (0, 1):
            total = total + ex2[way, c].astype(F32)
        wg_ref[2, c] = total.astype(BF16)

    scatter_sent(1)
    for i in (0, 1):
        for phase in (0, 1):
            for q in range(4):
                for copy in gather_copies(i, phase, q, stage):
                    copy.wait_send()
    for q in range(4):
        for copy in normed_copies(q):
            copy.wait_send()

    @pl.loop(0, hb)
    def _(c):
        for copy in list(ring_first(c) + ring_second(c)) + grad_copies(c):
            copy.wait_send()


def hand_over(seg_in, ing_in, wg_in, seg_out, ing_out, wg_out, seg_at, ing_at, wg_at, sem):
    pairs = [(seg_in, seg_at, seg_out), (ing_in, ing_at, ing_out)]
    for m in range(3):
        pairs.append((wg_in.at[0, m], wg_at.at[m], wg_out.at[0, m]))
    into = [pltpu.make_async_copy(a, b, sem.at[0, n]) for n, (a, b, _) in enumerate(pairs)]
    out = [pltpu.make_async_copy(b, c, sem.at[1, n]) for n, (_, b, c) in enumerate(pairs)]
    for copy in into:
        copy.start()
    for first, second in zip(into, out):
        first.wait()
        second.start()
    for copy in out:
        copy.wait()


def shards(inputs, cotangent, gains, weights, block_rows, block_count):
    n_dp, n_ts = lax.axis_size("dp"), lax.axis_size("ts")
    side = math.isqrt(n_ts)
    micro, shard_rows, width = inputs.shape
    rows = micro * shard_rows
    _, _, hb, slots, block, _ = weights.shape
    kb = width // block
    chunk = width // 4
    quarter = block // n_dp
    tokens = rows * n_ts
    vmem = pl.BlockSpec(memory_space=pltpu.VMEM)
    smem = pl.BlockSpec(memory_space=pltpu.SMEM)
    seg, ing, wg = pl.pallas_call(
        functools.partial(kernel, side, n_dp),
        out_shape=(
            jax.ShapeDtypeStruct((rows, width), BF16),
            jax.ShapeDtypeStruct((rows, width), BF16),
            jax.ShapeDtypeStruct((3, hb, slots, quarter, block), BF16),
        ),
        in_specs=[vmem, vmem, vmem, pl.BlockSpec(memory_space=pl.ANY), smem, smem],
        out_specs=(vmem, vmem, vmem),
        scratch_shapes=[
            pltpu.VMEM((hb, slots + 1, block, block), BF16),
            pltpu.VMEM((hb, slots + 1, block, block), BF16),
            pltpu.VMEM((hb, slots + 1, block, block), BF16),
            pltpu.VMEM((width, 2 * hb * block), BF16),
            pltpu.VMEM((hb * block, width), BF16),
            pltpu.VMEM((2, side, side, rows, width), BF16),
            pltpu.VMEM((side, side, rows, width), BF16),
            pltpu.VMEM((2, 4, side - 1, side, rows, chunk), BF16),
            pltpu.VMEM((2, 4, side - 1, rows, chunk), BF16),
            pltpu.VMEM((4, side, rows, chunk), BF16),
            pltpu.VMEM((rows, width), BF16),
            pltpu.VMEM((rows, width), BF16),
            pltpu.VMEM((1, width), F32),
            pltpu.VMEM((tokens, 2 * hb * block), F32),
            pltpu.VMEM((tokens, hb * block), F32),
            pltpu.VMEM((tokens, hb * block), BF16),
            pltpu.VMEM((hb, block, tokens), BF16),
            pltpu.VMEM((tokens, 2 * hb * block), BF16),
            pltpu.VMEM((3, tokens, 2 * hb * block), BF16),
            pltpu.VMEM((kb, block, tokens), BF16),
            pltpu.VMEM((4, kb, quarter, tokens), BF16),
            pltpu.VMEM((kb, tokens, block), BF16),
            pltpu.VMEM((2, hb, slots // 2, quarter, block), BF16),
            pltpu.VMEM((2, hb, slots, quarter, block), BF16),
            pltpu.SemaphoreType.DMA((3,)),
            pltpu.SemaphoreType.DMA((2, 2, 4, side)),
            pltpu.SemaphoreType.DMA((2, 2, 4, side)),
            pltpu.SemaphoreType.DMA((2, 2, 4, side - 1)),
            pltpu.SemaphoreType.DMA((2, 2, 4, side - 1)),
            pltpu.SemaphoreType.DMA((2,)),
            pltpu.SemaphoreType.DMA((2,)),
            pltpu.SemaphoreType.DMA((2, 2, hb)),
            pltpu.SemaphoreType.DMA((2, 2, hb)),
            pltpu.SemaphoreType.DMA((4, hb)),
            pltpu.SemaphoreType.DMA((4, hb)),
            pltpu.SemaphoreType.DMA((3, 4)),
            pltpu.SemaphoreType.DMA((3, 4)),
            pltpu.SemaphoreType.REGULAR((3,)),
            pltpu.VMEM((-(-3 * hb // 8) * 8, 128), jnp.int32),
            pltpu.SMEM((-(-3 * hb // 8) * 8, 128), jnp.int32),
            pltpu.SemaphoreType.DMA,
        ],
        compiler_params=pltpu.CompilerParams(
            collective_id=0, has_side_effects=True, vmem_limit_bytes=63 * 1024 * 1024
        ),
    )(
        inputs.reshape(rows, width),
        cotangent.reshape(rows, width),
        gains,
        weights[0],
        block_rows.transpose(1, 2, 0, 3),
        block_count.transpose(1, 0, 2),
    )
    shape = (1, micro, shard_rows, width)
    results = (seg.reshape(shape), ing.reshape(shape), wg[None])
    hbm = pl.BlockSpec(memory_space=pl.ANY)
    return pl.pallas_call(
        hand_over,
        out_shape=tuple(jax.ShapeDtypeStruct(x.shape, x.dtype) for x in results),
        in_specs=[hbm] * 3,
        out_specs=(hbm,) * 3,
        scratch_shapes=[
            pltpu.VMEM(shape, BF16),
            pltpu.VMEM(shape, BF16),
            pltpu.VMEM(wg.shape, BF16),
            pltpu.SemaphoreType.DMA((2, 5)),
        ],
    )(*results)


def solution(mesh):
    in_specs = (
        P(None, ("dp", "ts"), None),
        P(None, ("dp", "ts"), None),
        P("section", None),
        P("section", None, "ts", None, None, None),
        P("section", None, "ts", None),
        P("section", None, "ts"),
    )
    out_specs = (
        P("section", None, ("dp", "ts"), None),
        P("section", None, ("dp", "ts"), None),
        P("section", None, "ts", None, "dp", None),
    )
    return jax.shard_map(shards, mesh=mesh, in_specs=in_specs, out_specs=out_specs, check_vma=False)
```

```python
import functools
import math

import jax
import jax.numpy as jnp
from jax import lax
from jax.experimental import pallas as pl
from jax.experimental.pallas import tpu as pltpu
from jax.sharding import PartitionSpec as P

EPSILON = 1e-05
MESH = pl.DeviceIdType.MESH
F32 = jnp.float32
BF16 = jnp.bfloat16
NT = (((1,), (1,)), ((), ()))


def groups_of(hb):
    step = 2
    return [(lo, min(lo + step, hb)) for lo in range(0, hb, step)]


def kernel(
    side, n_dp,
    x_ref, cot_ref, gain_ref, w_hbm, rows_ref, count_ref,
    seg_ref, ing_ref, wg_ref,
    raw0, raw1, raw2, wgu, wd, g, part, rs1, rs2, mid, hop, stage, gain_x, gu, dhid, hid, hid_t, dgu, da, xt, xa, db, ex1, ex2,
    w_sem, ag_send, ag_recv, rs_send, rs_recv, hop_send, hop_recv, ex_send, ex_recv,
    da_send, da_recv, xa_send, xa_recv, go, inv_v, inv, inv_sem,
):
    rows, width = x_ref.shape
    chunk = width // 4
    _, hb, slots, block, _ = w_hbm.shape
    kb = width // block
    tokens = side * side * rows
    quarter = block // n_dp
    sec = lax.axis_index("section")
    ts = lax.axis_index("ts")
    me = lax.axis_index("dp")
    z, y = ts // side, lax.rem(ts, side)
    right, left = lax.rem(me + 1, n_dp), lax.rem(me + n_dp - 1, n_dp)
    across = lax.rem(me + 2, n_dp)
    raw = (raw0, raw1, raw2)
    cols = [slice(q * chunk, (q + 1) * chunk) for q in range(4)]
    halves = [slice(h * 2 * chunk, (h + 1) * 2 * chunk) for h in range(2)]
    order = (0, 2, 1, 3)
    groups = groups_of(hb)
    peers = [(lax.rem(z + d, side), lax.rem(y + d, side)) for d in range(side)]
    others = range(1, side)

    w_copies = [
        pltpu.make_async_copy(w_hbm.at[m], raw[m].at[:, pl.ds(0, slots)], w_sem.at[m])
        for m in range(3)
    ]
    for m in (2, 0, 1):
        w_copies[m].start()

    barrier = pltpu.get_barrier_semaphore()

    def greet(where):
        pl.semaphore_signal(barrier, inc=1, device_id=where, device_id_type=MESH)

    for d in others:
        pz, py = peers[d]
        for s in (0, 1):
            greet({"ts": pz * side + y, "section": s})
            greet({"ts": z * side + py, "section": s})
    for other in (right, left, across):
        greet({"dp": other})
    greet({"section": 1 - sec})

    def remote(src, dst, send, recv, where):
        return pltpu.make_async_remote_copy(
            src_ref=src, dst_ref=dst, send_sem=send, recv_sem=recv,
            device_id=where, device_id_type=MESH,
        )

    def gather_copies(i, phase, q, src=None):
        first = q < 2
        along_y = first == (phase == 0)
        copies = []
        for d in range(side):
            pz, py = peers[d]
            where = {"ts": z * side + py} if along_y else {"ts": pz * side + y}
            if phase == 0:
                dst = g.at[i, z, y, :, cols[q]]
                ref = dst
                if i == 1:
                    ref = src.at[:, cols[q]]
                    where["section"] = 1 - sec
                elif d == 0:
                    continue
            else:
                if d == 0:
                    continue
                ref = g.at[i, z, :, :, cols[q]] if first else g.at[i, :, y, :, cols[q]]
                dst = ref
            copies.append(remote(ref, dst, ag_send.at[i, phase, q, d], ag_recv.at[i, phase, q, d], where))
        return copies

    def gather_first(i, src=None):
        for q in order:
            for copy in gather_copies(i, 0, q, src):
                copy.start()

    def gather_second(i, some=order):
        for q in some:
            for copy in gather_copies(i, 0, q, stage):
                copy.wait_recv()
            for copy in gather_copies(i, 1, q):
                copy.start()

    def gather_end(i, q):
        for copy in gather_copies(i, 1, q):
            copy.wait_recv()

    def scatter_copies(use, phase, q):
        first = q < 2
        along_y = first == (phase == 1)
        copies = []
        for d in others:
            pz, py = peers[d]
            where = {"ts": z * side + py} if along_y else {"ts": pz * side + y}
            if phase == 0:
                src = part.at[pz, :, :, cols[q]] if first else part.at[:, py, :, cols[q]]
                dst = rs1.at[use, q, d - 1]
            else:
                src = mid.at[q, py if first else pz]
                dst = rs2.at[use, q, d - 1]
            copies.append(
                remote(src, dst, rs_send.at[use, phase, q, d - 1], rs_recv.at[use, phase, q, d - 1], where)
            )
        return copies

    def scatter_start(use, q):
        for copy in scatter_copies(use, 0, q):
            copy.start()

    def scatter_middle(use):
        for q in order:
            for copy in scatter_copies(use, 0, q):
                copy.wait_recv()
            for i in range(side):
                own = part[z, i, :, cols[q]] if q < 2 else part[i, y, :, cols[q]]
                total = own.astype(F32)
                for d in range(side - 1):
                    total = total + rs1[use, q, d, i].astype(F32)
                mid[q, i] = total.astype(BF16)
            for copy in scatter_copies(use, 1, q):
                copy.start()

    def scatter_end(use):
        totals = []
        for q in range(4):
            for copy in scatter_copies(use, 1, q):
                copy.wait_recv()
            total = mid[q, y if q < 2 else z].astype(F32)
            for d in range(side - 1):
                total = total + rs2[use, q, d].astype(F32)
            totals.append(total)
        return jnp.concatenate(totals, axis=1)

    def scatter_sent(use):
        for phase in (0, 1):
            for q in range(4):
                for copy in scatter_copies(use, phase, q):
                    copy.wait_send()

    def scale_of(values):
        return lax.rsqrt(jnp.mean(values * values, axis=-1, keepdims=True) + EPSILON)

    def normed_of(values, gain):
        return (values * scale_of(values) * gain).astype(BF16)

    def wide(i, q):
        return g[i, :, :, :, cols[q]].reshape(tokens, chunk)

    def act_copy():
        return remote(seg_ref, hop, hop_send.at[0], hop_recv.at[0], {"section": 1})

    def gain_copy():
        return remote(gain_ref, gain_x, hop_send.at[1], hop_recv.at[1], {"section": 0})

    @pl.when(sec == 0)
    def _():
        g[0, z, y] = normed_of(x_ref[...].astype(F32), gain_ref[...])

    @pl.when(sec == 1)
    def _():
        g[0, z, y] = cot_ref[...]

    pl.semaphore_wait(barrier, 4 * (side - 1) + 4)
    gather_first(0)

    @pl.when(sec == 1)
    def _():
        gain_copy().start()

    for m in range(3):
        raw[m][:, slots] = jnp.zeros((hb, block, block), BF16)

    lane = lax.broadcasted_iota(jnp.int32, (1, inv_v.shape[1]), 1)
    for m in range(3):
        for c in range(hb):
            found = jnp.full(lane.shape, slots, jnp.int32)
            for j in range(slots):
                row = jnp.where(j < count_ref[m, 0, c], rows_ref[m, c, 0, j], -1)
                found = jnp.where(lane == row, j, found)
            inv_v[pl.ds(m * hb + c, 1), :] = found
    inv_copy = pltpu.make_async_copy(inv_v, inv, inv_sem)
    inv_copy.start()
    inv_copy.wait()
    w_copies[2].wait()

    @pl.loop(0, kb)
    def _(k):
        column = pl.ds(pl.multiple_of(k * block, block), block)
        for c in range(hb):
            slot = inv[2 * hb + c, k]
            wd[c * block : (c + 1) * block, column] = raw[2][c, slot]

    @pl.when(sec == 0)
    def _():
        gather_second(0)

    w_copies[0].wait()
    w_copies[1].wait()

    @pl.loop(0, kb)
    def _(k):
        for m in range(2):
            for c in range(hb):
                slot = inv[m * hb + c, k]
                at = (2 * c + m) * block
                wgu[pl.ds(k * block, block), at : at + block] = raw[m][c, slot]

    per_chunk = chunk // block

    def quarter_of(q):
        return pl.ds(pl.multiple_of(q * quarter, quarter), quarter)

    def normed_copies(q):
        part_of = pl.ds(q * per_chunk, per_chunk)
        return [
            remote(
                xt.at[part_of, quarter_of(to)], xa.at[n + 1, part_of],
                xa_send.at[n, q], xa_recv.at[n, q], {"dp": to},
            )
            for n, to in enumerate((right, left, across))
        ]

    def transposed(i, q):
        @pl.loop(0, per_chunk)
        def _(k):
            column = pl.ds(pl.multiple_of(q * chunk + k * block, block), block)
            xt[q * per_chunk + k] = g[i, :, :, :, column].reshape(tokens, block).T
            xa[0, q * per_chunk + k] = xt[q * per_chunk + k, quarter_of(me), :]

        for copy in normed_copies(q):
            copy.start()

    def delta_blocks(i, q):
        @pl.loop(0, per_chunk)
        def _(k):
            column = pl.ds(pl.multiple_of(q * chunk + k * block, block), block)
            db[q * per_chunk + k] = g[i, :, :, :, column].reshape(tokens, block)

    def down_grad_input(i, some=order):
        for n, q in enumerate(some):
            gather_end(i, q)
            term = lax.dot_general(wide(i, q), wd[:, cols[q]], NT, preferred_element_type=F32)
            dhid[...] = term if q == order[0] else dhid[...] + term
            delta_blocks(i, q)

    def allow(n):
        pl.semaphore_signal(go.at[n], inc=1, device_id={"section": 1}, device_id_type=MESH)

    def gate_and_up(i):
        for n, q in enumerate(order):
            gather_end(i, q)
            term = jnp.dot(wide(i, q), wgu[cols[q], :], preferred_element_type=F32)
            gu[...] = term if n == 0 else gu[...] + term
            if i == 1 and n < 3:
                transposed(i, q)

    @pl.when(sec == 0)
    def _():
        gate_and_up(0)
        allow(0)

    @pl.when(sec == 1)
    def _():
        pl.semaphore_wait(go.at[0], 1)
        gather_second(0, order[:2])
        down_grad_input(0, order[:2])
        pl.semaphore_wait(go.at[1], 1)
        gather_second(0, order[2:])
        down_grad_input(0, order[2:])
        gather_second(1)
        gate_and_up(1)

    def gate_of(c):
        at = pl.multiple_of(c * 2 * block, 2 * block)
        return gu[:, pl.ds(at, block)], gu[:, pl.ds(pl.multiple_of(at + block, block), block)]

    def hidden():
        @pl.loop(0, hb)
        def _(c):
            gate, upper = gate_of(c)
            hid[:, pl.ds(pl.multiple_of(c * block, block), block)] = (
                gate * jax.nn.sigmoid(gate) * upper
            ).astype(BF16)

    def hidden_transposed(some):
        for q in some:
            transposed(sec, q)

        @pl.loop(0, hb)
        def _(c):
            hid_t[c] = hid[:, pl.ds(pl.multiple_of(c * block, block), block)].T

    def down(use):
        for q in order:
            out = jnp.dot(hid[...], wd[:, cols[q]], preferred_element_type=F32)
            part[:, :, :, cols[q]] = out.astype(BF16).reshape(side, side, rows, chunk)
            scatter_start(use, q)

    def back(use):
        for q in order:
            out = lax.dot_general(dgu[...], wgu[cols[q], :], NT, preferred_element_type=F32)
            part[:, :, :, cols[q]] = out.astype(BF16).reshape(side, side, rows, chunk)
            scatter_start(use, q)

    def input_grad(values, delta, d_norm):
        scale = scale_of(values)
        scaled = gain_ref[...] * d_norm
        spread = jnp.mean(scaled * values, axis=-1, keepdims=True)
        return (delta + scale * scaled - values * (scale * scale * scale) * spread).astype(BF16)

    def pre_activation_grads(n):
        @pl.loop(*groups[n])
        def _(c):
            gate, upper = gate_of(c)
            d_hidden = dhid[:, pl.ds(pl.multiple_of(c * block, block), block)]
            sig = jax.nn.sigmoid(gate)
            d_gate = d_hidden * upper * sig * (1.0 + gate * (1.0 - sig))
            d_up = d_hidden * gate * sig
            at = pl.multiple_of(c * 2 * block, 2 * block)
            dgu[:, pl.ds(at, block)] = d_gate.astype(BF16)
            dgu[:, pl.ds(pl.multiple_of(at + block, block), block)] = d_up.astype(BF16)

    def grad_copies(group, which):
        lo, hi = groups[group]
        col = slice(lo * 2 * block, hi * 2 * block)
        low, high = pl.ds(0, tokens // 2), pl.ds(tokens // 2, tokens // 2)
        moves = (
            (dgu.at[:, col], da.at[0, :, col], right),
            (dgu.at[:, col], da.at[1, :, col], left),
            (da.at[0, low, col], da.at[2, low, col], right),
            (da.at[1, high, col], da.at[2, high, col], left),
        )
        return [
            remote(src, dst, da_send.at[n, group], da_recv.at[n, group], {"dp": to})
            for n, (src, dst, to) in enumerate(moves)
            if n in which
        ]

    def grads_out(group):
        for copy in grad_copies(group, (0, 1)):
            copy.start()

    def relay():
        for group in range(len(groups)):
            for n in (0, 1):
                grad_copies(group, (n,))[0].wait_recv()
                grad_copies(group, (n + 2,))[0].start()

    first, second = slice(0, slots // 2), slice(slots // 2, slots)

    def ring_first(group):
        q, here = quarter_of(across), slice(*groups[group])
        return (
            remote(raw2.at[here, first, q], ex1.at[0, here], ex_send.at[0, 0, group], ex_recv.at[0, 0, group], {"dp": right}),
            remote(raw2.at[here, second, q], ex1.at[1, here], ex_send.at[0, 1, group], ex_recv.at[0, 1, group], {"dp": left}),
        )

    def ring_second(group):
        here, every = slice(*groups[group]), slice(0, slots)
        return (
            remote(raw2.at[here, every, quarter_of(right)], ex2.at[0, here], ex_send.at[1, 0, group], ex_recv.at[1, 0, group], {"dp": right}),
            remote(raw2.at[here, every, quarter_of(left)], ex2.at[1, here], ex_send.at[1, 1, group], ex_recv.at[1, 1, group], {"dp": left}),
        )

    def pass_on():
        for group in range(len(groups)):
            for copy in ring_first(group):
                copy.wait_recv()

            @pl.loop(*groups[group])
            def _(c):
                for into, which, arrived in ((right, first, 0), (left, second, 1)):
                    q = quarter_of(into)
                    mine = raw2[c, which, q, :].astype(F32)
                    raw2[c, which, q, :] = (mine + ex1[arrived, c].astype(F32)).astype(BF16)

            for copy in ring_second(group):
                copy.start()

    def live_of(m, c, j):
        return (j < count_ref[m, 0, c]).astype(F32)

    def down_weight_grads():
        for group in range(len(groups)):
            @pl.loop(*groups[group])
            def _(c):
                picked = [db[rows_ref[2, c, 0, j]] for j in range(slots)]
                out = jnp.dot(hid_t[c], jnp.concatenate(picked, axis=1), preferred_element_type=F32)
                for j in range(slots):
                    raw2[c, j] = (out[:, j * block : (j + 1) * block] * live_of(2, c, j)).astype(BF16)

            for copy in ring_first(group):
                copy.start()

    def weight_grads():
        for q in range(4):
            for copy in normed_copies(q):
                copy.wait_recv()
        for group in range(len(groups)):
            for copy in grad_copies(group, (2, 3)):
                copy.wait_recv()

            @pl.loop(*groups[group])
            def _(c):
                for m in range(2):
                    col = pl.ds(pl.multiple_of((2 * c + m) * block, block), block)
                    grads = jnp.concatenate([dgu[:, col]] + [da[n, :, col] for n in range(3)], axis=0)
                    picked = []
                    for j in range(slots):
                        row = rows_ref[m, c, 0, j]
                        picked.append(jnp.concatenate([xa[n, row] for n in range(4)], axis=1))
                    out = jnp.dot(jnp.concatenate(picked, axis=0), grads, preferred_element_type=F32)
                    for j in range(slots):
                        wg_ref[m, c, j] = (out[j * quarter : (j + 1) * quarter] * live_of(m, c, j)).astype(BF16)

    @pl.when(sec == 0)
    def _():
        hidden()
        down(0)
        hidden_transposed(order)
        gain_copy().wait_recv()
        scatter_middle(0)
        allow(1)
        act = (x_ref[...].astype(F32) + scatter_end(0)).astype(BF16)
        seg_ref[...] = act
        stage[...] = normed_of(act.astype(F32), gain_x[...])
        gather_first(1, stage)
        act_copy().start()
        scatter_sent(0)
        gather_second(1)
        down_grad_input(1)
        allow(2)
        for group in range(len(groups)):
            pre_activation_grads(group)
            grads_out(group)
        down_weight_grads()
        back(1)
        relay()
        pass_on()
        scatter_middle(1)
        weight_grads()
        ing_ref[...] = input_grad(x_ref[...].astype(F32), g[1, z, y].astype(F32), scatter_end(1))
        act_copy().wait_send()

    @pl.when(sec == 1)
    def _():
        for group in range(len(groups)):
            pre_activation_grads(group)
            grads_out(group)
        back(0)
        hidden()
        hidden_transposed(order[3:])
        down_weight_grads()
        act_copy().wait_recv()
        scatter_middle(0)
        relay()
        ing_ref[...] = input_grad(hop[...].astype(F32), cot_ref[...].astype(F32), scatter_end(0))
        stage[...] = ing_ref[...]
        gather_first(1, stage)
        scatter_sent(0)
        pass_on()
        weight_grads()
        pl.semaphore_wait(go.at[2], 1)
        down(1)
        scatter_middle(1)
        seg_ref[...] = (hop[...].astype(F32) + scatter_end(1)).astype(BF16)
        gain_copy().wait_send()

    for group in range(len(groups)):
        for copy in ring_second(group):
            copy.wait_recv()

        @pl.loop(*groups[group])
        def _(c):
            total = raw2[c, pl.ds(0, slots), quarter_of(me), :].astype(F32)
            for way in (0, 1):
                total = total + ex2[way, c].astype(F32)
            wg_ref[2, c] = total.astype(BF16)

    scatter_sent(1)
    for i in (0, 1):
        for phase in (0, 1):
            for q in range(4):
                for copy in gather_copies(i, phase, q, stage):
                    copy.wait_send()
    for q in range(4):
        for copy in normed_copies(q):
            copy.wait_send()
    for group in range(len(groups)):
        for copy in list(ring_first(group) + ring_second(group)) + grad_copies(group, (0, 1, 2, 3)):
            copy.wait_send()


def hand_over(seg_in, ing_in, wg_in, seg_out, ing_out, wg_out, seg_at, ing_at, wg_at, sem):
    pairs = [(seg_in, seg_at, seg_out), (ing_in, ing_at, ing_out)]
    for m in range(3):
        pairs.append((wg_in.at[0, m], wg_at.at[m], wg_out.at[0, m]))
    into = [pltpu.make_async_copy(a, b, sem.at[0, n]) for n, (a, b, _) in enumerate(pairs)]
    out = [pltpu.make_async_copy(b, c, sem.at[1, n]) for n, (_, b, c) in enumerate(pairs)]
    for copy in into:
        copy.start()
    for first, second in zip(into, out):
        first.wait()
        second.start()
    for copy in out:
        copy.wait()


def shards(inputs, cotangent, gains, weights, block_rows, block_count):
    n_dp, n_ts = lax.axis_size("dp"), lax.axis_size("ts")
    side = math.isqrt(n_ts)
    micro, shard_rows, width = inputs.shape
    rows = micro * shard_rows
    _, _, hb, slots, block, _ = weights.shape
    kb = width // block
    chunk = width // 4
    quarter = block // n_dp
    tokens = rows * n_ts
    vmem = pl.BlockSpec(memory_space=pltpu.VMEM)
    smem = pl.BlockSpec(memory_space=pltpu.SMEM)
    seg, ing, wg = pl.pallas_call(
        functools.partial(kernel, side, n_dp),
        out_shape=(
            jax.ShapeDtypeStruct((rows, width), BF16),
            jax.ShapeDtypeStruct((rows, width), BF16),
            jax.ShapeDtypeStruct((3, hb, slots, quarter, block), BF16),
        ),
        in_specs=[vmem, vmem, vmem, pl.BlockSpec(memory_space=pl.ANY), smem, smem],
        out_specs=(vmem, vmem, vmem),
        scratch_shapes=[
            pltpu.VMEM((hb, slots + 1, block, block), BF16),
            pltpu.VMEM((hb, slots + 1, block, block), BF16),
            pltpu.VMEM((hb, slots + 1, block, block), BF16),
            pltpu.VMEM((width, 2 * hb * block), BF16),
            pltpu.VMEM((hb * block, width), BF16),
            pltpu.VMEM((2, side, side, rows, width), BF16),
            pltpu.VMEM((side, side, rows, width), BF16),
            pltpu.VMEM((2, 4, side - 1, side, rows, chunk), BF16),
            pltpu.VMEM((2, 4, side - 1, rows, chunk), BF16),
            pltpu.VMEM((4, side, rows, chunk), BF16),
            pltpu.VMEM((rows, width), BF16),
            pltpu.VMEM((rows, width), BF16),
            pltpu.VMEM((1, width), F32),
            pltpu.VMEM((tokens, 2 * hb * block), F32),
            pltpu.VMEM((tokens, hb * block), F32),
            pltpu.VMEM((tokens, hb * block), BF16),
            pltpu.VMEM((hb, block, tokens), BF16),
            pltpu.VMEM((tokens, 2 * hb * block), BF16),
            pltpu.VMEM((3, tokens, 2 * hb * block), BF16),
            pltpu.VMEM((kb, block, tokens), BF16),
            pltpu.VMEM((4, kb, quarter, tokens), BF16),
            pltpu.VMEM((kb, tokens, block), BF16),
            pltpu.VMEM((2, hb, slots // 2, quarter, block), BF16),
            pltpu.VMEM((2, hb, slots, quarter, block), BF16),
            pltpu.SemaphoreType.DMA((3,)),
            pltpu.SemaphoreType.DMA((2, 2, 4, side)),
            pltpu.SemaphoreType.DMA((2, 2, 4, side)),
            pltpu.SemaphoreType.DMA((2, 2, 4, side - 1)),
            pltpu.SemaphoreType.DMA((2, 2, 4, side - 1)),
            pltpu.SemaphoreType.DMA((2,)),
            pltpu.SemaphoreType.DMA((2,)),
            pltpu.SemaphoreType.DMA((2, 2, len(groups_of(hb)))),
            pltpu.SemaphoreType.DMA((2, 2, len(groups_of(hb)))),
            pltpu.SemaphoreType.DMA((4, len(groups_of(hb)))),
            pltpu.SemaphoreType.DMA((4, len(groups_of(hb)))),
            pltpu.SemaphoreType.DMA((3, 4)),
            pltpu.SemaphoreType.DMA((3, 4)),
            pltpu.SemaphoreType.REGULAR((3,)),
            pltpu.VMEM((-(-3 * hb // 8) * 8, 128), jnp.int32),
            pltpu.SMEM((-(-3 * hb // 8) * 8, 128), jnp.int32),
            pltpu.SemaphoreType.DMA,
        ],
        compiler_params=pltpu.CompilerParams(
            collective_id=0, has_side_effects=True, vmem_limit_bytes=63 * 1024 * 1024
        ),
    )(
        inputs.reshape(rows, width),
        cotangent.reshape(rows, width),
        gains,
        weights[0],
        block_rows.transpose(1, 2, 0, 3),
        block_count.transpose(1, 0, 2),
    )
    shape = (1, micro, shard_rows, width)
    results = (seg.reshape(shape), ing.reshape(shape), wg[None])
    hbm = pl.BlockSpec(memory_space=pl.ANY)
    return pl.pallas_call(
        hand_over,
        out_shape=tuple(jax.ShapeDtypeStruct(x.shape, x.dtype) for x in results),
        in_specs=[hbm] * 3,
        out_specs=(hbm,) * 3,
        scratch_shapes=[
            pltpu.VMEM(shape, BF16),
            pltpu.VMEM(shape, BF16),
            pltpu.VMEM(wg.shape, BF16),
            pltpu.SemaphoreType.DMA((2, 5)),
        ],
    )(*results)


def solution(mesh):
    in_specs = (
        P(None, ("dp", "ts"), None),
        P(None, ("dp", "ts"), None),
        P("section", None),
        P("section", None, "ts", None, None, None),
        P("section", None, "ts", None),
        P("section", None, "ts"),
    )
    out_specs = (
        P("section", None, ("dp", "ts"), None),
        P("section", None, ("dp", "ts"), None),
        P("section", None, "ts", None, "dp", None),
    )
    return jax.shard_map(shards, mesh=mesh, in_specs=in_specs, out_specs=out_specs, check_vma=False)
```
